256 devices in a mesh: blk: 32 (over y_lo, z, core), rep: 8 (over y_hi, x).
Axes of the slice: x: 4, y: 4 (y_hi: 2, y_lo: 2; y = y_hi * 2 + y_lo), z: 8, core: 2. Of those that a mesh axis runs over, the one named last changes fastest.
Arguments:
- tokens: bfloat16 [32768, 4096], P(('blk', 'rep')), may hold values from -24 to 24
- cotangent: bfloat16 [32768, 4096], P(('blk', 'rep')), may hold values from -1.5 to 1.5
- gate_weight: bfloat16 [4096, 11008], P(None, 'blk'), may hold values from -0.25 to 0.25
- up_weight: bfloat16 [4096, 11008], P(None, 'blk'), may hold values from -0.25 to 0.25
- down_weight: bfloat16 [11008, 4096], P('blk'), may hold values from -0.0546875 to 0.0546875
Outputs:
- input_grad: bfloat16 [32768, 4096], P(('blk', 'rep'))
- gate_grad: bfloat16 [4096, 11008], P('rep', 'blk')
- up_grad: bfloat16 [4096, 11008], P('rep', 'blk')
- down_grad: bfloat16 [11008, 4096], P('blk', 'rep')
The draws below stay inside these ranges and needn't reach their ends.
All inputs are finite; a program needn't handle non-finite values.
Results may differ from the reference program's by a relative error of at most 0.019.
Values may be sent and summed in bfloat16 or wider, within the bound.
No kernel may reach another device: no remote copies, remote signals or barrier semaphores. Data moves between devices by JAX's collectives and lax.ppermute only.
A program may use at most 128 MiB of HBM per device.

```python
import jax
import jax.numpy as jnp
from jax import lax

D = 4096
FF = 11008
TOK_DEV = 128
TOKENS = 32768
N_BLK = 32
N_REP = 8


def with_spikes(drawn, own_key, source, target, parts, factor):
    owner, partner = [(jnp.arange(drawn.shape[axis_at]) // (drawn.shape[axis_at] // parts)).reshape([-1 if axis == axis_at else 1 for axis in range(drawn.ndim)]) for axis_at in (source, target)]
    chosen = jax.random.permutation(own_key, parts)[partner]
    strong = (owner == chosen) | (owner == (partner + parts // 2) % parts)
    return jnp.where(strong, factor * drawn, drawn)


def levels(own_key, shape, split, low, high):
    def one(position, blocks):
        draws = jax.random.uniform(jax.random.fold_in(jax.random.fold_in(own_key, 6), position), (blocks,), jnp.float32, low / len(split), high / len(split))
        return jnp.repeat(jnp.exp(draws), shape[position] // blocks).reshape((-1,) + (1,) * (len(shape) - position - 1))

    loudness = one(*split[0])
    for cut in split[1:]:
        loudness = loudness * one(*cut)
    return loudness


def noise(own_key, dims, spread, most, pieces=(), kind=jnp.bfloat16):
    values = spread * jax.random.normal(own_key, dims, jnp.float32)
    if pieces:
        values = values * levels(own_key, dims, pieces, -0.22, 0.18)
    return jnp.clip(values, -most, most).astype(kind)


def gaussian_with(key, shape, scale, limit, shards, heavy, kind=jnp.bfloat16):
    array = scale * jax.random.normal(key, shape, jnp.float32)
    if shards:
        array = array * levels(key, shape, shards, -0.22, 0.18)
    return jnp.clip(with_spikes(array, jax.random.fold_in(key, 3), *heavy), -limit, limit).astype(kind)


def setup_inputs(seed: int = 0) -> dict:
    seeds = jax.random.split(jax.random.key(seed), 6)
    tokens = gaussian_with(seeds[0], (TOKENS, D), 1.0, 24.0, ((0, 256),), (0, 1, 256, 6.0))
    cotangent = noise(seeds[1], (TOKENS, D), 0.25, 1.5, ((0, 256),))
    gate_weight = noise(seeds[2], (D, FF), (D // 8) ** -0.5, 0.25, ((1, 32),))
    up_weight = noise(seeds[3], (D, FF), (D // 8) ** -0.5, 0.25, ((1, 32),))
    down_weight = noise(seeds[4], (FF, D), FF ** -0.5, 0.0546875, ((0, 32),))
    return dict(tokens=tokens, cotangent=cotangent, gate_weight=gate_weight, up_weight=up_weight, down_weight=down_weight)


def contract_rows(left, right):
    return lax.dot_general(left, right, (((0,), (0,)), ((), ())), preferred_element_type=jnp.float32)


def contract_cols(left, right):
    return lax.dot_general(left, right, (((1,), (1,)), ((), ())), preferred_element_type=jnp.float32)


def shard_terms(rows, cotan, w_gate, w_up, w_down):
    gate = jnp.dot(rows, w_gate, preferred_element_type=jnp.float32)
    upval = jnp.dot(rows, w_up, preferred_element_type=jnp.float32)
    sigma = jax.nn.sigmoid(gate)
    active = gate * sigma
    slope = sigma * (1.0 + gate * (1.0 - sigma))
    hidden = (active * upval).astype(jnp.bfloat16)
    d_hidden = contract_cols(cotan, w_down)
    d_up = (d_hidden * active).astype(jnp.bfloat16)
    d_gate = (d_hidden * upval * slope).astype(jnp.bfloat16)
    term_x = contract_cols(d_gate, w_gate) + contract_cols(d_up, w_up)
    grad_gate = contract_rows(rows, d_gate).astype(jnp.bfloat16)
    grad_up = contract_rows(rows, d_up).astype(jnp.bfloat16)
    grad_down = contract_rows(hidden, cotan).astype(jnp.bfloat16)
    return term_x, grad_gate, grad_up, grad_down


def reference(tokens, cotangent, gate_weight, up_weight, down_weight):
    width = FF // N_BLK
    dx_init = jnp.zeros((TOKENS, D), jnp.float32)
    gg_init = jnp.zeros((D, FF), jnp.float32)
    gu_init = jnp.zeros((D, FF), jnp.float32)
    gd_init = jnp.zeros((FF, D), jnp.float32)

    def per_block(carry, blk_id):
        col = (blk_id * width).astype(jnp.int32)
        w_gate = lax.dynamic_slice_in_dim(gate_weight, col, width, 1)
        w_up = lax.dynamic_slice_in_dim(up_weight, col, width, 1)
        w_down = lax.dynamic_slice_in_dim(down_weight, col, width, 0)
        nxt = ((blk_id + 1) % N_BLK).astype(jnp.int32)

        def per_rep(inner, rep_id):
            dx_acc, gg, gu, gd = inner
            own_start = ((blk_id * N_REP + rep_id) * TOK_DEV).astype(jnp.int32)
            far_start = ((nxt * N_REP + rep_id) * TOK_DEV).astype(jnp.int32)
            own_rows = lax.dynamic_slice_in_dim(tokens, own_start, TOK_DEV, 0)
            own_cot = lax.dynamic_slice_in_dim(cotangent, own_start, TOK_DEV, 0)
            far_rows = lax.dynamic_slice_in_dim(tokens, far_start, TOK_DEV, 0)
            far_cot = lax.dynamic_slice_in_dim(cotangent, far_start, TOK_DEV, 0)
            ax, ag, au, ad = shard_terms(own_rows, own_cot, w_gate, w_up, w_down)
            bx, bg, bu, bd = shard_terms(far_rows, far_cot, w_gate, w_up, w_down)
            ag, au, ad, bg, bu, bd = lax.optimization_barrier((ag, au, ad, bg, bu, bd))
            pair_g = (ag.astype(jnp.float32) + bg.astype(jnp.float32)).astype(jnp.bfloat16)
            pair_u = (au.astype(jnp.float32) + bu.astype(jnp.float32)).astype(jnp.bfloat16)
            pair_d = (ad.astype(jnp.float32) + bd.astype(jnp.float32)).astype(jnp.bfloat16)
            pair_g, pair_u, pair_d = lax.optimization_barrier((pair_g, pair_u, pair_d))
            zero = jnp.zeros((), jnp.int32)
            gg = lax.dynamic_update_slice(gg, lax.dynamic_slice_in_dim(gg, col, width, 1) + pair_g.astype(jnp.float32), (zero, col))
            gu = lax.dynamic_update_slice(gu, lax.dynamic_slice_in_dim(gu, col, width, 1) + pair_u.astype(jnp.float32), (zero, col))
            gd = lax.dynamic_update_slice(gd, lax.dynamic_slice_in_dim(gd, col, width, 0) + pair_d.astype(jnp.float32), (col, zero))
            dx_acc = lax.dynamic_update_slice(dx_acc, lax.dynamic_slice_in_dim(dx_acc, own_start, TOK_DEV, 0) + ax, (own_start, zero))
            dx_acc = lax.dynamic_update_slice(dx_acc, lax.dynamic_slice_in_dim(dx_acc, far_start, TOK_DEV, 0) + bx, (far_start, zero))
            return (dx_acc, gg, gu, gd), None

        carry, _ = lax.scan(per_rep, carry, jnp.arange(N_REP, dtype=jnp.int32))
        return carry, None

    (dx_acc, gg, gu, gd), _ = lax.scan(per_block, (dx_init, gg_init, gu_init, gd_init), jnp.arange(N_BLK, dtype=jnp.int32))
    return (dx_acc.astype(jnp.bfloat16), gg.astype(jnp.bfloat16), gu.astype(jnp.bfloat16), gd.astype(jnp.bfloat16))
```

```python
import jax
import jax.numpy as jnp
from jax import lax
from jax.sharding import PartitionSpec as P

ROW = 4


def along_blk(value, by):
    size = lax.axis_size("blk")
    return lax.ppermute(value, "blk", [(i, (i + by) % size) for i in range(size)])


def partner(r, j, i):
    return (r // ROW ^ j) * ROW + (r % ROW + i) % ROW


def along_rep(value, j, i):
    return lax.ppermute(value, "rep", [(r, partner(r, j, i)) for r in range(2 * ROW)])


def nt(left, right):
    return lax.dot_general(
        left, right, (((1,), (1,)), ((), ())), preferred_element_type=jnp.float32
    )


def tn(left, right):
    return lax.dot_general(
        left, right, (((0,), (0,)), ((), ())), preferred_element_type=jnp.float32
    )


def unit_grads(rows, cotan, w_gate, w_up, w_down):
    gate = nt(w_gate, rows)
    upval = nt(w_up, rows)
    sigma = jax.nn.sigmoid(gate)
    active = gate * sigma
    slope = sigma * (1.0 + gate * (1.0 - sigma))
    hidden = (active * upval).astype(jnp.bfloat16)
    d_hidden = nt(w_down, cotan)
    d_up = (d_hidden * active).astype(jnp.bfloat16)
    d_gate = (d_hidden * upval * slope).astype(jnp.bfloat16)
    return jnp.concatenate([d_gate, d_up, hidden])


def row_term(grads, w_gate, w_up):
    s = w_gate.shape[0]
    return tn(grads[:s], w_gate) + tn(grads[s : 2 * s], w_up)


def local(tokens, cotangent, gate_weight, up_weight, down_weight):
    w_gate, w_up, w_down = gate_weight.T, up_weight.T, down_weight
    s = w_gate.shape[0]
    far_rows = along_blk(tokens, -1)
    far_cotan = along_blk(cotangent, -1)
    me = lax.axis_index("rep")
    wide = tokens.shape[1] // (2 * ROW)

    def columns(i):
        out = []
        for j in range(2):
            to = (me // ROW ^ j) * ROW + (me % ROW + i) % ROW
            out += [lax.dynamic_slice_in_dim(a, to * wide, wide, 1) for a in (tokens, cotangent)]
        return jnp.concatenate(out, 1)

    near_cols = jnp.concatenate([columns(0)] + [along_rep(columns(i), 0, i) for i in range(1, ROW)])
    far_cols = along_blk(near_cols, -1)

    own = unit_grads(tokens, cotangent, w_gate, w_up, w_down)
    own_all = [own] + [along_rep(own, 0, i) for i in range(1, ROW)]
    own_x = row_term(own, w_gate, w_up)

    far = unit_grads(far_rows, far_cotan, w_gate, w_up, w_down)
    far_all = [far] + [along_rep(far, 0, i) for i in range(1, ROW)]
    far_x = row_term(far, w_gate, w_up).astype(jnp.bfloat16)

    grads = jnp.concatenate(own_all + far_all, 1)
    cols = jnp.concatenate([near_cols, far_cols])

    def weight_terms(first):
        pair = jnp.dot(grads[: 2 * s], cols[:, first : first + wide], preferred_element_type=jnp.float32)
        down = jnp.dot(grads[2 * s :], cols[:, first + wide : first + 2 * wide], preferred_element_type=jnp.float32)
        return pair, down

    other = jnp.concatenate([a.astype(jnp.bfloat16) for a in weight_terms(2 * wide)])
    other = along_rep(other, 1, 0).astype(jnp.float32)
    pair, down = weight_terms(0)
    pair = (pair + other[: 2 * s]).astype(jnp.bfloat16)
    down = (down + other[2 * s :]).astype(jnp.bfloat16)
    input_grad = (own_x + along_blk(far_x, 1).astype(jnp.float32)).astype(jnp.bfloat16)
    return input_grad, pair[:s].T, pair[s:].T, down


def solution(mesh):
    in_specs = (
        P(("blk", "rep"), None),
        P(("blk", "rep"), None),
        P(None, "blk"),
        P(None, "blk"),
        P("blk", None),
    )
    out_specs = (P(("blk", "rep"), None), P("rep", "blk"), P("rep", "blk"), P("blk", "rep"))
    return jax.shard_map(local, mesh=mesh, in_specs=in_specs, out_specs=out_specs, check_vma=False)
```

```python
import functools

import jax
import jax.numpy as jnp
from jax import lax
from jax.experimental import pallas as pl
from jax.experimental.pallas import tpu as pltpu
from jax.sharding import PartitionSpec as P

ROW = 4
HALF = 176
STEPS = 4
MIB = 1 << 20


def along_blk(value, by):
    size = lax.axis_size("blk")
    return lax.ppermute(value, "blk", [(i, (i + by) % size) for i in range(size)])


def partner(r, j, i):
    return (r // ROW ^ j) * ROW + (r % ROW + i) % ROW


def along_rep(value, j, i):
    return lax.ppermute(value, "rep", [(r, partner(r, j, i)) for r in range(2 * ROW)])


def nt(left, right):
    return lax.dot_general(
        left, right, (((1,), (1,)), ((), ())), preferred_element_type=jnp.float32
    )


def tn(left, right):
    return lax.dot_general(
        left, right, (((0,), (0,)), ((), ())), preferred_element_type=jnp.float32
    )


def cost(us):
    return pl.CostEstimate(flops=int(us * 1e9), bytes_accessed=int(us * 3.5e6), transcendentals=0)


def params():
    return pltpu.CompilerParams(vmem_limit_bytes=40 * MIB)


def halves(d_gate, d_up, hidden):
    pad = jnp.zeros((2 * HALF - d_gate.shape[0], d_gate.shape[1]), jnp.float32)
    parts = (d_gate, d_up, hidden)
    first = jnp.concatenate([p[:HALF] for p in parts])
    second = jnp.concatenate([q for p in parts for q in (p[HALF:], pad)])
    return first.astype(jnp.bfloat16), second.astype(jnp.bfloat16)


def unit_grads(gate, upval, d_hidden):
    sigma = jax.nn.sigmoid(gate)
    active = gate * sigma
    slope = sigma * (1.0 + gate * (1.0 - sigma))
    return halves(d_hidden * upval * slope, d_hidden * active, active * upval)


VMEM = pl.BlockSpec(memory_space=pltpu.VMEM)


def deep(weight, rows):
    wide = weight.shape[1] // STEPS
    return sum(nt(weight[:, k * wide : (k + 1) * wide], rows[:, k * wide : (k + 1) * wide]) for k in range(STEPS))


def own_kernel(x, c, wg, wu, wd, first, second):
    first[...], second[...] = unit_grads(deep(wg, x), deep(wu, x), deep(wd, c))


def own_units(x, c, wg, wu, wd, us):
    t = x.shape[0]
    return pl.pallas_call(
        own_kernel,
        in_specs=[VMEM] * 5,
        out_specs=[VMEM] * 2,
        out_shape=[jax.ShapeDtypeStruct((3 * HALF, t), jnp.bfloat16)] * 2,
        compiler_params=params(),
        cost_estimate=cost(us),
        name="own_units",
    )(x, c, wg, wu, wd)


def gate_up_kernel(x, wg, wu, gate, upval):
    gate[...] = deep(wg, x)
    upval[...] = deep(wu, x)


def gate_up(x, wg, wu, us):
    return pl.pallas_call(
        gate_up_kernel,
        in_specs=[VMEM] * 3,
        out_specs=[VMEM] * 2,
        out_shape=[jax.ShapeDtypeStruct((wg.shape[0], x.shape[0]), jnp.float32)] * 2,
        compiler_params=params(),
        cost_estimate=cost(us),
        name="gate_up",
    )(x, wg, wu)


def far_kernel(c, wd, gate, upval, own_first, own_second, first, second):
    t = c.shape[0]
    first[:, :t] = own_first[...]
    second[:, :t] = own_second[...]
    first[:, t:], second[:, t:] = unit_grads(gate[...], upval[...], deep(wd, c))


def far_units(c, wd, gate, upval, own_first, own_second, us):
    return pl.pallas_call(
        far_kernel,
        in_specs=[VMEM] * 6,
        out_specs=[VMEM] * 2,
        out_shape=[jax.ShapeDtypeStruct((3 * HALF, 2 * c.shape[0]), jnp.bfloat16)] * 2,
        compiler_params=params(),
        cost_estimate=cost(us),
        name="far_units",
    )(c, wd, gate, upval, own_first, own_second)


def term_kernel(at, first, second, wg, wu, out):
    s, d = wg.shape
    cols = slice(at, at + out.shape[0])
    grads = []
    for n in range(2):
        rows = slice(n * HALF, (n + 1) * HALF)
        grads.append(jnp.concatenate([first[rows, cols], second[rows, cols]])[:s])
    for k in range(STEPS):
        cut = slice(k * d // STEPS, (k + 1) * d // STEPS)
        out[:, cut] = (tn(grads[0], wg[:, cut]) + tn(grads[1], wu[:, cut])).astype(out.dtype)


def row_term(first, second, wg, wu, at, t, dtype, us):
    return pl.pallas_call(
        functools.partial(term_kernel, at),
        in_specs=[VMEM] * 4,
        out_specs=VMEM,
        out_shape=jax.ShapeDtypeStruct((t, wg.shape[1]), dtype),
        compiler_params=params(),
        cost_estimate=cost(us),
        name="row_term",
    )(first, second, wg, wu)


def pack_kernel(x, c, *refs):
    outs, sem = refs[:-1], refs[-1]
    me = lax.axis_index("rep")
    wide = x.shape[1] // (2 * ROW)
    copies = []
    for i, out in enumerate(outs):
        for j in range(2):
            row = lax.rem(me // ROW + j, 2)
            to = row * ROW + lax.rem(me + i, ROW)
            source = pl.ds(pl.multiple_of(to * wide, wide), wide)
            for n, a in enumerate((x, c)):
                target = pl.ds((2 * j + n) * wide, wide)
                copies.append(pltpu.make_async_copy(a.at[:, source], out.at[:, target], sem.at[len(copies)]))
    for copy in copies:
        copy.start()
    for copy in copies:
        copy.wait()


def pack(x, c, pieces, us):
    t, d = x.shape
    return pl.pallas_call(
        pack_kernel,
        out_shape=[jax.ShapeDtypeStruct((t, d // 2), jnp.bfloat16)] * pieces,
        in_specs=[pl.BlockSpec(memory_space=pl.ANY)] * 2,
        out_specs=[pl.BlockSpec(memory_space=pl.ANY)] * pieces,
        scratch_shapes=[pltpu.SemaphoreType.DMA((4 * pieces,))],
        compiler_params=params(),
        cost_estimate=cost(us),
        name="pack",
    )(x, c)


def weight_kernel(at, *refs):
    near, far, grads, out = refs[:ROW], refs[ROW : ROW + 2], refs[ROW + 2 : -1], refs[-1]
    t = near[0].shape[0]
    wide = out.shape[1]
    left = jnp.concatenate([g[...] for g in grads], 1)

    def columns(first):
        cut = slice(first, first + wide)
        tall = [a for i in range(ROW) for a in (
            near[i][:, cut],
            far[0][:, cut] if i == 0 else far[1][(i - 1) * t : i * t, cut],
        )]
        return jnp.concatenate(tall)

    dot = functools.partial(jnp.dot, preferred_element_type=jnp.float32)
    out[: 2 * HALF] = dot(left[: 2 * HALF], columns(at)).astype(out.dtype)
    out[2 * HALF :] = dot(left[2 * HALF :], columns(at + wide)).astype(out.dtype)


def weight_terms(near, far, grads, at, dtype, us):
    wide = near[0].shape[1] // 4
    return pl.pallas_call(
        functools.partial(weight_kernel, at * wide),
        out_shape=jax.ShapeDtypeStruct((3 * HALF, wide), dtype),
        in_specs=[VMEM] * (2 * ROW + 2),
        out_specs=VMEM,
        compiler_params=params(),
        cost_estimate=cost(us),
        name="weight_terms",
    )(*near, *far, *grads)


def sum_kernel(a, b, a_other, b_other, gate, up, down):
    s = gate.shape[0]
    for n, out in enumerate((gate, up, down)):
        rows = slice(n * HALF, (n + 1) * HALF)
        total = a[rows] + a_other[rows].astype(jnp.float32)
        out[:HALF] = total.astype(out.dtype)
        total = b[rows] + b_other[rows].astype(jnp.float32)
        out[HALF:] = total[: s - HALF].astype(out.dtype)


def sums(a, b, a_other, b_other, s):
    return pl.pallas_call(
        sum_kernel,
        out_shape=[jax.ShapeDtypeStruct((s, a.shape[1]), jnp.bfloat16)] * 3,
        in_specs=[VMEM] * 4,
        out_specs=[VMEM] * 3,
        compiler_params=params(),
        cost_estimate=cost(1),
        name="sums",
    )(a, b, a_other, b_other)


def local(tokens, cotangent, gate_weight, up_weight, down_weight):
    w_gate, w_up, w_down = gate_weight.T, up_weight.T, down_weight
    s = w_gate.shape[0]
    t = tokens.shape[0]
    far_rows = along_blk(tokens, -1)
    far_cotan = along_blk(cotangent, -1)
    in_hbm = [pltpu.with_memory_space_constraint(a, pltpu.HBM) for a in (tokens, cotangent)]
    near = pack(*in_hbm, ROW, 1)
    near = [near[0]] + [along_rep(near[i], 0, i) for i in range(1, ROW)]

    own = own_units(tokens, cotangent, w_gate, w_up, w_down, 20)
    own_x = row_term(*own, w_gate, w_up, 0, t, jnp.float32, 3)

    far_rows, own_x = lax.optimization_barrier((far_rows, own_x))
    gate, upval = gate_up(far_rows, w_gate, w_up, 2)
    both = far_units(far_cotan, w_down, gate, upval, *own, 1.5)
    far_x = row_term(*both, w_gate, w_up, t, t, jnp.bfloat16, 1)
    near, far_x = lax.optimization_barrier((near, far_x))
    far_x = along_blk(far_x, 1)
    first, second = both
    second, far_x = lax.optimization_barrier((second, far_x))
    gathered = [[g] + [along_rep(g, 0, i) for i in range(1, ROW)] for g in (first, second)]
    far_cols = along_blk(jnp.concatenate(near[1:]), -1)
    far = [pack(far_rows, far_cotan, 1, 0.5)[0], far_cols]

    other = [along_rep(weight_terms(near, far, g, 2, jnp.bfloat16, 1), 1, 0) for g in gathered]
    mine = [weight_terms(near, far, g, 0, jnp.float32, 1) for g in gathered]
    gate_grad, up_grad, down_grad = sums(*mine, *other, s)
    input_grad = (own_x + far_x.astype(jnp.float32)).astype(jnp.bfloat16)
    return input_grad, gate_grad.T, up_grad.T, down_grad


def solution(mesh):
    in_specs = (
        P(("blk", "rep"), None),
        P(("blk", "rep"), None),
        P(None, "blk"),
        P(None, "blk"),
        P("blk", None),
    )
    out_specs = (P(("blk", "rep"), None), P("rep", "blk"), P("rep", "blk"), P("blk", "rep"))
    return jax.shard_map(local, mesh=mesh, in_specs=in_specs, out_specs=out_specs, check_vma=False)
```

```python
import functools

import jax
import jax.numpy as jnp
from jax import lax
from jax.experimental import pallas as pl
from jax.experimental.pallas import tpu as pltpu
from jax.sharding import PartitionSpec as P

ROW = 4
CUT = 176
PADDED = 352
STEPS = 4
MIB = 1 << 20


def along_blk(value, by):
    size = lax.axis_size("blk")
    return lax.ppermute(value, "blk", [(i, (i + by) % size) for i in range(size)])


def partner(r, j, i):
    return (r // ROW ^ j) * ROW + (r % ROW + i) % ROW


def along_rep(value, j, i):
    return lax.ppermute(value, "rep", [(r, partner(r, j, i)) for r in range(2 * ROW)])


def nt(left, right):
    return lax.dot_general(
        left, right, (((1,), (1,)), ((), ())), preferred_element_type=jnp.float32
    )


def tn(left, right):
    return lax.dot_general(
        left, right, (((0,), (0,)), ((), ())), preferred_element_type=jnp.float32
    )


def cost(us):
    return pl.CostEstimate(flops=int(us * 1e9), bytes_accessed=int(us * 3.5e6), transcendentals=0)


def params():
    return pltpu.CompilerParams(vmem_limit_bytes=40 * MIB)


def halves(d_gate, d_up, hidden):
    pad = jnp.zeros((PADDED - d_gate.shape[0], d_gate.shape[1]), jnp.float32)
    parts = (d_gate, d_up, hidden)
    first = jnp.concatenate([p[:CUT] for p in parts])
    second = jnp.concatenate([q for p in parts for q in (p[CUT:], pad)])
    return first.astype(jnp.bfloat16), second.astype(jnp.bfloat16)


def unit_grads(gate, upval, d_hidden):
    sigma = jax.nn.sigmoid(gate)
    active = gate * sigma
    slope = sigma * (1.0 + gate * (1.0 - sigma))
    return halves(d_hidden * upval * slope, d_hidden * active, active * upval)


VMEM = pl.BlockSpec(memory_space=pltpu.VMEM)


def deep(weight, rows):
    wide = weight.shape[1] // STEPS
    return sum(nt(weight[:, k * wide : (k + 1) * wide], rows[:, k * wide : (k + 1) * wide]) for k in range(STEPS))


def own_kernel(x, c, wg, wu, wd, first, second):
    first[...], second[...] = unit_grads(deep(wg, x), deep(wu, x), deep(wd, c))


def own_units(x, c, wg, wu, wd, us):
    t = x.shape[0]
    return pl.pallas_call(
        own_kernel,
        in_specs=[VMEM] * 5,
        out_specs=[VMEM] * 2,
        out_shape=[jax.ShapeDtypeStruct((3 * n, t), jnp.bfloat16) for n in (CUT, PADDED - CUT)],
        compiler_params=params(),
        cost_estimate=cost(us),
        name="own_units",
    )(x, c, wg, wu, wd)


def gate_up_kernel(x, wg, wu, gate, upval):
    gate[...] = deep(wg, x)
    upval[...] = deep(wu, x)


def gate_up(x, wg, wu, us):
    return pl.pallas_call(
        gate_up_kernel,
        in_specs=[VMEM] * 3,
        out_specs=[VMEM] * 2,
        out_shape=[jax.ShapeDtypeStruct((wg.shape[0], x.shape[0]), jnp.float32)] * 2,
        compiler_params=params(),
        cost_estimate=cost(us),
        name="gate_up",
    )(x, wg, wu)


def far_kernel(c, wd, gate, upval, own_first, own_second, first, second):
    t = c.shape[0]
    first[:, :t] = own_first[...]
    second[:, :t] = own_second[...]
    first[:, t:], second[:, t:] = unit_grads(gate[...], upval[...], deep(wd, c))


def far_units(c, wd, gate, upval, own_first, own_second, us):
    return pl.pallas_call(
        far_kernel,
        in_specs=[VMEM] * 6,
        out_specs=[VMEM] * 2,
        out_shape=[jax.ShapeDtypeStruct((3 * n, 2 * c.shape[0]), jnp.bfloat16) for n in (CUT, PADDED - CUT)],
        compiler_params=params(),
        cost_estimate=cost(us),
        name="far_units",
    )(c, wd, gate, upval, own_first, own_second)


def term_kernel(at, first, second, wg, wu, out):
    s, d = wg.shape
    cols = slice(at, at + out.shape[0])
    grads = []
    for n in range(2):
        parts = [a[n * a.shape[0] // 3 : (n + 1) * a.shape[0] // 3, cols] for a in (first, second)]
        grads.append(jnp.concatenate(parts)[:s])
    for k in range(STEPS):
        cut = slice(k * d // STEPS, (k + 1) * d // STEPS)
        out[:, cut] = (tn(grads[0], wg[:, cut]) + tn(grads[1], wu[:, cut])).astype(out.dtype)


def row_term(first, second, wg, wu, at, t, dtype, us):
    return pl.pallas_call(
        functools.partial(term_kernel, at),
        in_specs=[VMEM] * 4,
        out_specs=VMEM,
        out_shape=jax.ShapeDtypeStruct((t, wg.shape[1]), dtype),
        compiler_params=params(),
        cost_estimate=cost(us),
        name="row_term",
    )(first, second, wg, wu)


def pack_kernel(x, c, *refs):
    outs, sem = refs[:-1], refs[-1]
    me = lax.axis_index("rep")
    wide = x.shape[1] // (2 * ROW)
    copies = []
    for i, out in enumerate(outs):
        for j in range(2):
            row = lax.rem(me // ROW + 1 + j, 2)
            to = row * ROW + lax.rem(me + i, ROW)
            source = pl.ds(pl.multiple_of(to * wide, wide), wide)
            for n, a in enumerate((x, c)):
                target = pl.ds((2 * j + n) * wide, wide)
                copies.append(pltpu.make_async_copy(a.at[:, source], out.at[:, target], sem.at[len(copies)]))
    for copy in copies:
        copy.start()
    for copy in copies:
        copy.wait()


def pack(x, c, pieces, us):
    t, d = x.shape
    return pl.pallas_call(
        pack_kernel,
        out_shape=[jax.ShapeDtypeStruct((t, d // 2), jnp.bfloat16)] * pieces,
        in_specs=[pl.BlockSpec(memory_space=pl.ANY)] * 2,
        out_specs=[pl.BlockSpec(memory_space=pl.ANY)] * pieces,
        scratch_shapes=[pltpu.SemaphoreType.DMA((4 * pieces,))],
        compiler_params=params(),
        cost_estimate=cost(us),
        name="pack",
    )(x, c)


def weight_kernel(at, *refs):
    near, head, tail, grads, out = refs[:ROW], refs[ROW], refs[ROW + 1], refs[ROW + 2 : -1], refs[-1]
    t = near[0].shape[0]
    n, wide = out.shape[0] // 3, out.shape[1]
    left = jnp.concatenate([g[...] for g in grads], 1)

    def columns(first):
        parts = [near[0][:, at + first : at + first + wide], head[:, at + first : at + first + wide]]
        for i in range(1, ROW):
            parts.append(near[i][:, at + first : at + first + wide])
            parts.append(tail[(i - 1) * t : i * t, first : first + wide])
        return jnp.concatenate(parts)

    dot = functools.partial(jnp.dot, preferred_element_type=jnp.float32)
    out[: 2 * n] = dot(left[: 2 * n], columns(0)).astype(out.dtype)
    out[2 * n :] = dot(left[2 * n :], columns(wide)).astype(out.dtype)


def weight_terms(near, head, tail, grads, at, dtype, us):
    wide = near[0].shape[1] // 4
    return pl.pallas_call(
        functools.partial(weight_kernel, at * wide),
        out_shape=jax.ShapeDtypeStruct((grads[0].shape[0], wide), dtype),
        in_specs=[VMEM] * (2 * ROW + 2),
        out_specs=VMEM,
        compiler_params=params(),
        cost_estimate=cost(us),
        name="weight_terms",
    )(*near, head, tail, *grads)


def sum_kernel(first, second, first_other, second_other, gate, up, down):
    s = gate.shape[0]
    for n, out in enumerate((gate, up, down)):
        for a, b, at in ((first, first_other, 0), (second, second_other, CUT)):
            part = a.shape[0] // 3
            rows = slice(n * part, (n + 1) * part)
            total = a[rows] + b[rows].astype(jnp.float32)
            out[at : min(at + part, s)] = total[: s - at].astype(out.dtype)


def sums(first, second, first_other, second_other, s):
    return pl.pallas_call(
        sum_kernel,
        out_shape=[jax.ShapeDtypeStruct((s, first.shape[1]), jnp.bfloat16)] * 3,
        in_specs=[VMEM] * 4,
        out_specs=[VMEM] * 3,
        compiler_params=params(),
        cost_estimate=cost(1),
        name="sums",
    )(first, second, first_other, second_other)


def local(tokens, cotangent, gate_weight, up_weight, down_weight):
    w_gate, w_up, w_down = gate_weight.T, up_weight.T, down_weight
    s = w_gate.shape[0]
    t = tokens.shape[0]
    far_rows = along_blk(tokens, -1)
    in_hbm = [pltpu.with_memory_space_constraint(a, pltpu.HBM) for a in (tokens, cotangent)]
    near = list(pack(*in_hbm, ROW, 1))
    late, near[0] = lax.optimization_barrier((cotangent, near[0]))
    far_cotan = along_blk(late, -1)
    near = [near[0]] + [along_rep(near[i], 0, i) for i in range(1, ROW)]

    own = own_units(tokens, cotangent, w_gate, w_up, w_down, 20)
    own_x = row_term(*own, w_gate, w_up, 0, t, jnp.float32, 3)

    far_rows, own_x = lax.optimization_barrier((far_rows, own_x))
    gate, upval = gate_up(far_rows, w_gate, w_up, 2)
    both = far_units(far_cotan, w_down, gate, upval, *own, 1.5)
    far_x = row_term(*both, w_gate, w_up, t, t, jnp.bfloat16, 1)
    near, far_x = lax.optimization_barrier((near, far_x))
    half = near[0].shape[1] // 2
    far_other = along_blk(jnp.concatenate([a[:, :half] for a in near[1:]]), -1)
    far_x = along_blk(far_x, 1)
    first, second = ([g] + [along_rep(g, 0, i) for i in (1, 3)] for g in both)
    first.insert(2, along_rep(first[1], 0, 1))
    second.insert(2, along_rep(second[2], 0, 3))
    own_cols = near[1:]
    far_mine = along_blk(jnp.concatenate([a[:, half:] for a in own_cols]), -1)
    far = pack(far_rows, far_cotan, 1, 0.5)[0]

    other = [along_rep(weight_terms(near, far, far_other, g, 0, jnp.bfloat16, 1), 1, 0) for g in (first, second)]
    mine = [weight_terms(near, far, far_mine, g, 2, jnp.float32, 1) for g in (first, second)]
    gate_grad, up_grad, down_grad = sums(*mine, *other, s)
    input_grad = (own_x + far_x.astype(jnp.float32)).astype(jnp.bfloat16)
    return input_grad, gate_grad.T, up_grad.T, down_grad


def solution(mesh):
    in_specs = (
        P(("blk", "rep"), None),
        P(("blk", "rep"), None),
        P(None, "blk"),
        P(None, "blk"),
        P("blk", None),
    )
    out_specs = (P(("blk", "rep"), None), P("rep", "blk"), P("rep", "blk"), P("blk", "rep"))
    return jax.shard_map(local, mesh=mesh, in_specs=in_specs, out_specs=out_specs, check_vma=False)
```

```python
import functools

import jax
import jax.numpy as jnp
from jax import lax
from jax.experimental import pallas as pl
from jax.experimental.pallas import tpu as pltpu
from jax.sharding import PartitionSpec as P

ROW = 4
CUT = 176
STEPS = 4
MIB = 1 << 20


def along_blk(value, by):
    size = lax.axis_size("blk")
    return lax.ppermute(value, "blk", [(i, (i + by) % size) for i in range(size)])


def partner(r, j, i):
    return (r // ROW ^ j) * ROW + (r % ROW + i) % ROW


def along_rep(value, j, i):
    return lax.ppermute(value, "rep", [(r, partner(r, j, i)) for r in range(2 * ROW)])


def nt(left, right):
    return lax.dot_general(
        left, right, (((1,), (1,)), ((), ())), preferred_element_type=jnp.float32
    )


def tn(left, right):
    return lax.dot_general(
        left, right, (((0,), (0,)), ((), ())), preferred_element_type=jnp.float32
    )


def cost(us):
    return pl.CostEstimate(flops=int(us * 1e9), bytes_accessed=int(us * 3.5e6), transcendentals=0)


def params():
    return pltpu.CompilerParams(vmem_limit_bytes=40 * MIB)


def halves(d_gate, d_up, hidden):
    parts = (d_gate, d_up, hidden)
    first = jnp.concatenate([p[:CUT] for p in parts])
    second = jnp.concatenate([p[CUT:] for p in parts])
    return first.astype(jnp.bfloat16), second.astype(jnp.bfloat16)


def unit_grads(gate, upval, d_hidden):
    sigma = jax.nn.sigmoid(gate)
    active = gate * sigma
    slope = sigma * (1.0 + gate * (1.0 - sigma))
    return halves(d_hidden * upval * slope, d_hidden * active, active * upval)


VMEM = pl.BlockSpec(memory_space=pltpu.VMEM)


def deep(weight, rows):
    wide = weight.shape[1] // STEPS
    return sum(nt(weight[:, k * wide : (k + 1) * wide], rows[:, k * wide : (k + 1) * wide]) for k in range(STEPS))


def own_kernel(x, c, wg, wu, wd, first, second):
    first[...], second[...] = unit_grads(deep(wg, x), deep(wu, x), deep(wd, c))


def own_units(x, c, wg, wu, wd, us):
    t = x.shape[0]
    return pl.pallas_call(
        own_kernel,
        in_specs=[VMEM] * 5,
        out_specs=[VMEM] * 2,
        out_shape=[jax.ShapeDtypeStruct((3 * n, t), jnp.bfloat16) for n in (CUT, wg.shape[0] - CUT)],
        compiler_params=params(),
        cost_estimate=cost(us),
        name="own_units",
    )(x, c, wg, wu, wd)


def gate_up_kernel(x, wg, wu, gate, upval):
    gate[...] = deep(wg, x)
    upval[...] = deep(wu, x)


def gate_up(x, wg, wu, us):
    return pl.pallas_call(
        gate_up_kernel,
        in_specs=[VMEM] * 3,
        out_specs=[VMEM] * 2,
        out_shape=[jax.ShapeDtypeStruct((wg.shape[0], x.shape[0]), jnp.float32)] * 2,
        compiler_params=params(),
        cost_estimate=cost(us),
        name="gate_up",
    )(x, wg, wu)


def far_kernel(c, wd, gate, upval, own_first, own_second, first, second, both):
    t = c.shape[0]
    far = unit_grads(gate[...], upval[...], deep(wd, c))
    first[:, :t] = own_first[...]
    first[:, t:] = far[0]
    second[:, :t] = own_second[...]
    second[:, t:] = far[1]
    both[: 3 * CUT] = first[...]
    both[3 * CUT :] = second[...]


def far_units(c, wd, gate, upval, own_first, own_second, us):
    return pl.pallas_call(
        far_kernel,
        in_specs=[VMEM] * 6,
        out_specs=[VMEM] * 3,
        out_shape=[
            jax.ShapeDtypeStruct((3 * n, 2 * c.shape[0]), jnp.bfloat16)
            for n in (CUT, wd.shape[0] - CUT, wd.shape[0])
        ],
        compiler_params=params(),
        cost_estimate=cost(us),
        name="far_units",
    )(c, wd, gate, upval, own_first, own_second)


def term_kernel(at, first, second, wg, wu, out):
    s, d = wg.shape
    cols = slice(at, at + out.shape[0])
    wide = [a[:, cols].astype(jnp.float32) for a in (first, second)]
    grads = []
    for n in range(2):
        parts = [a[n * a.shape[0] // 3 : (n + 1) * a.shape[0] // 3] for a in wide]
        grads.append(jnp.concatenate(parts).astype(jnp.bfloat16))
    for k in range(STEPS):
        cut = slice(k * d // STEPS, (k + 1) * d // STEPS)
        out[:, cut] = (tn(grads[0], wg[:, cut]) + tn(grads[1], wu[:, cut])).astype(out.dtype)


def row_term(first, second, wg, wu, at, t, dtype, us):
    return pl.pallas_call(
        functools.partial(term_kernel, at),
        in_specs=[VMEM] * 4,
        out_specs=VMEM,
        out_shape=jax.ShapeDtypeStruct((t, wg.shape[1]), dtype),
        compiler_params=params(),
        cost_estimate=cost(us),
        name="row_term",
    )(first, second, wg, wu)


def pack_kernel(first, x, c, *refs):
    outs, sem = refs[:-1], refs[-1]
    me = lax.axis_index("rep")
    wide = x.shape[1] // (2 * ROW)
    copies = []
    for i, out in enumerate(outs, first):
        for j in range(2):
            row = lax.rem(me // ROW + 1 + j, 2)
            to = row * ROW + lax.rem(me + i, ROW)
            source = pl.ds(pl.multiple_of(to * wide, wide), wide)
            for n, a in enumerate((x, c)):
                target = pl.ds((2 * j + n) * wide, wide)
                copies.append(pltpu.make_async_copy(a.at[:, source], out.at[:, target], sem.at[len(copies)]))
    for copy in copies:
        copy.start()
    for copy in copies:
        copy.wait()


def pack(x, c, first, pieces, us):
    t, d = x.shape
    return pl.pallas_call(
        functools.partial(pack_kernel, first),
        out_shape=[jax.ShapeDtypeStruct((t, d // 2), jnp.bfloat16)] * pieces,
        in_specs=[pl.BlockSpec(memory_space=pl.ANY)] * 2,
        out_specs=[pl.BlockSpec(memory_space=pl.ANY)] * pieces,
        scratch_shapes=[pltpu.SemaphoreType.DMA((4 * pieces,))],
        compiler_params=params(),
        cost_estimate=cost(us),
        name="pack",
    )(x, c)


def weight_kernel(at, *refs):
    near, head, tail, grads, out = refs[:ROW], refs[ROW], refs[ROW + 1], refs[ROW + 2 : -1], refs[-1]
    t = near[0].shape[0]
    n, wide = out.shape[0] // 3, out.shape[1]
    left = jnp.concatenate([g[...] for g in grads], 1)

    def columns(first):
        parts = [near[0][:, at + first : at + first + wide], head[:, at + first : at + first + wide]]
        for i in range(1, ROW):
            parts.append(near[i][:, at + first : at + first + wide])
            parts.append(tail[(i - 1) * t : i * t, first : first + wide])
        return jnp.concatenate(parts)

    dot = functools.partial(jnp.dot, preferred_element_type=jnp.float32)
    out[: 2 * n] = dot(left[: 2 * n], columns(0)).astype(out.dtype)
    out[2 * n :] = dot(left[2 * n :], columns(wide)).astype(out.dtype)


def weight_terms(near, head, tail, grads, at, dtype, us):
    wide = near[0].shape[1] // 4
    return pl.pallas_call(
        functools.partial(weight_kernel, at * wide),
        out_shape=jax.ShapeDtypeStruct((grads[0].shape[0], wide), dtype),
        in_specs=[VMEM] * (2 * ROW + 2),
        out_specs=VMEM,
        compiler_params=params(),
        cost_estimate=cost(us),
        name="weight_terms",
    )(*near, head, tail, *grads)


def sum_kernel(first, second, first_other, second_other, gate, up, down):
    for a, b, at in ((first, first_other, 0), (second, second_other, CUT)):
        part = a.shape[0] // 3
        total = a[...] + b[...].astype(jnp.float32)
        for n, out in enumerate((gate, up, down)):
            out[at : at + part] = total[n * part : (n + 1) * part].astype(out.dtype)


def sums(first, second, first_other, second_other, s):
    return pl.pallas_call(
        sum_kernel,
        out_shape=[jax.ShapeDtypeStruct((s, first.shape[1]), jnp.bfloat16)] * 3,
        in_specs=[VMEM] * 4,
        out_specs=[VMEM] * 3,
        compiler_params=params(),
        cost_estimate=cost(1),
        name="sums",
    )(first, second, first_other, second_other)


def local(tokens, cotangent, gate_weight, up_weight, down_weight):
    w_gate, w_up, w_down = gate_weight.T, up_weight.T, down_weight
    s = w_gate.shape[0]
    t = tokens.shape[0]
    far_rows = along_blk(tokens, -1)
    in_hbm = [pltpu.with_memory_space_constraint(a, pltpu.HBM) for a in (tokens, cotangent)]
    near = [None, *pack(*in_hbm, 1, ROW - 1, 1)]
    late, near[1] = lax.optimization_barrier((cotangent, near[1]))
    far_cotan = along_blk(late, -1)
    near = [along_rep(near[i], 0, i) for i in range(1, ROW)]

    own = own_units(tokens, cotangent, w_gate, w_up, w_down, 20)
    own_x = row_term(*own, w_gate, w_up, 0, t, jnp.float32, 3)

    far_rows, own_x = lax.optimization_barrier((far_rows, own_x))
    gate, upval = gate_up(far_rows, w_gate, w_up, 2)
    first, second, both = far_units(far_cotan, w_down, gate, upval, *own, 1.5)
    far_x = row_term(first, second, w_gate, w_up, t, t, jnp.bfloat16, 1)
    near, far_x = lax.optimization_barrier((near, far_x))
    half = near[0].shape[1] // 2
    late, far_cotan = lax.optimization_barrier((cotangent, far_cotan))
    far_other = along_blk(jnp.concatenate([a[:, :half] for a in near]), -1)
    far_x = along_blk(far_x, 1)
    both = along_rep(both, 0, 3)
    first = [first, along_rep(first, 0, 1)]
    first += [along_rep(first[1], 0, 1), both[: 3 * CUT]]
    second = [second, along_rep(second, 0, 1), along_rep(both[3 * CUT :], 0, 3), both[3 * CUT :]]
    far_mine = along_blk(jnp.concatenate([a[:, half:] for a in near]), -1)
    far = pack(far_rows, far_cotan, 0, 1, 0.5)[0]
    near = [pack(tokens, late, 0, 1, 0.5)[0], *near]

    other = [along_rep(weight_terms(near, far, far_other, g, 0, jnp.bfloat16, 1), 1, 0) for g in (first, second)]
    mine = [weight_terms(near, far, far_mine, g, 2, jnp.float32, 1) for g in (first, second)]
    gate_grad, up_grad, down_grad = sums(*mine, *other, s)
    input_grad = (own_x + far_x.astype(jnp.float32)).astype(jnp.bfloat16)
    return input_grad, gate_grad.T, up_grad.T, down_grad


def solution(mesh):
    in_specs = (
        P(("blk", "rep"), None),
        P(("blk", "rep"), None),
        P(None, "blk"),
        P(None, "blk"),
        P("blk", None),
    )
    out_specs = (P(("blk", "rep"), None), P("rep", "blk"), P("rep", "blk"), P("blk", "rep"))
    return jax.shard_map(local, mesh=mesh, in_specs=in_specs, out_specs=out_specs, check_vma=False)
```

```python
import functools

import jax
import jax.numpy as jnp
from jax import lax
from jax.experimental import pallas as pl
from jax.experimental.pallas import tpu as pltpu
from jax.sharding import PartitionSpec as P

ROW = 4
CUT = 176
STEPS = 4
MIB = 1 << 20


def along_blk(value, by):
    size = lax.axis_size("blk")
    return lax.ppermute(value, "blk", [(i, (i + by) % size) for i in range(size)])


def partner(r, j, i):
    return (r // ROW ^ j) * ROW + (r % ROW + i) % ROW


def along_rep(value, j, i):
    return lax.ppermute(value, "rep", [(r, partner(r, j, i)) for r in range(2 * ROW)])


def nt(left, right):
    return lax.dot_general(
        left, right, (((1,), (1,)), ((), ())), preferred_element_type=jnp.float32
    )


def tn(left, right):
    return lax.dot_general(
        left, right, (((0,), (0,)), ((), ())), preferred_element_type=jnp.float32
    )


def cost(us):
    return pl.CostEstimate(flops=int(us * 1e9), bytes_accessed=int(us * 3.5e6), transcendentals=0)


def params():
    return pltpu.CompilerParams(vmem_limit_bytes=40 * MIB)


def halves(d_gate, d_up, hidden):
    parts = (d_gate, d_up, hidden)
    first = jnp.concatenate([p[:CUT] for p in parts])
    second = jnp.concatenate([p[CUT:] for p in parts])
    return first.astype(jnp.bfloat16), second.astype(jnp.bfloat16)


def unit_grads(gate, upval, d_hidden):
    sigma = jax.nn.sigmoid(gate)
    active = gate * sigma
    slope = sigma * (1.0 + gate * (1.0 - sigma))
    return halves(d_hidden * upval * slope, d_hidden * active, active * upval)


VMEM = pl.BlockSpec(memory_space=pltpu.VMEM)


def deep(weight, rows):
    wide = weight.shape[1] // STEPS
    return sum(nt(weight[:, k * wide : (k + 1) * wide], rows[:, k * wide : (k + 1) * wide]) for k in range(STEPS))


def own_kernel(x, c, wg, wu, wd, first, second):
    first[...], second[...] = unit_grads(deep(wg, x), deep(wu, x), deep(wd, c))


def own_units(x, c, wg, wu, wd, us):
    t = x.shape[0]
    return pl.pallas_call(
        own_kernel,
        in_specs=[VMEM] * 5,
        out_specs=[VMEM] * 2,
        out_shape=[jax.ShapeDtypeStruct((3 * n, t), jnp.bfloat16) for n in (CUT, wg.shape[0] - CUT)],
        compiler_params=params(),
        cost_estimate=cost(us),
        name="own_units",
    )(x, c, wg, wu, wd)


def gate_up_kernel(x, wg, wu, gate, upval):
    gate[...] = deep(wg, x)
    upval[...] = deep(wu, x)


def gate_up(x, wg, wu, us):
    return pl.pallas_call(
        gate_up_kernel,
        in_specs=[VMEM] * 3,
        out_specs=[VMEM] * 2,
        out_shape=[jax.ShapeDtypeStruct((wg.shape[0], x.shape[0]), jnp.float32)] * 2,
        compiler_params=params(),
        cost_estimate=cost(us),
        name="gate_up",
    )(x, wg, wu)


def far_kernel(c, wd, gate, upval, own_first, own_second, first, second, both):
    t = c.shape[0]
    far = unit_grads(gate[...], upval[...], deep(wd, c))
    first[:, :t] = own_first[...]
    first[:, t:] = far[0]
    second[:, :t] = own_second[...]
    second[:, t:] = far[1]
    both[: 3 * CUT] = first[...]
    both[3 * CUT :] = second[...]


def far_units(c, wd, gate, upval, own_first, own_second, us):
    return pl.pallas_call(
        far_kernel,
        in_specs=[VMEM] * 6,
        out_specs=[VMEM] * 3,
        out_shape=[
            jax.ShapeDtypeStruct((3 * n, 2 * c.shape[0]), jnp.bfloat16)
            for n in (CUT, wd.shape[0] - CUT, wd.shape[0])
        ],
        compiler_params=params(),
        cost_estimate=cost(us),
        name="far_units",
    )(c, wd, gate, upval, own_first, own_second)


def term_kernel(at, first, second, wg, wu, out):
    s, d = wg.shape
    cols = slice(at, at + out.shape[0])
    wide = [a[:, cols].astype(jnp.float32) for a in (first, second)]
    grads = []
    for n in range(2):
        parts = [a[n * a.shape[0] // 3 : (n + 1) * a.shape[0] // 3] for a in wide]
        grads.append(jnp.concatenate(parts).astype(jnp.bfloat16))
    for k in range(STEPS):
        cut = slice(k * d // STEPS, (k + 1) * d // STEPS)
        out[:, cut] = (tn(grads[0], wg[:, cut]) + tn(grads[1], wu[:, cut])).astype(out.dtype)


def row_term(first, second, wg, wu, at, t, dtype, us):
    return pl.pallas_call(
        functools.partial(term_kernel, at),
        in_specs=[VMEM] * 4,
        out_specs=VMEM,
        out_shape=jax.ShapeDtypeStruct((t, wg.shape[1]), dtype),
        compiler_params=params(),
        cost_estimate=cost(us),
        name="row_term",
    )(first, second, wg, wu)


def pack_kernel(first, x, c, *refs):
    outs, sem = refs[:-1], refs[-1]
    me = lax.axis_index("rep")
    wide = x.shape[1] // (2 * ROW)
    copies = []
    for i, out in enumerate(outs, first):
        for j in range(2):
            row = lax.rem(me // ROW + 1 + j, 2)
            to = row * ROW + lax.rem(me + i, ROW)
            source = pl.ds(pl.multiple_of(to * wide, wide), wide)
            for n, a in enumerate((x, c)):
                target = pl.ds((2 * j + n) * wide, wide)
                copies.append(pltpu.make_async_copy(a.at[:, source], out.at[:, target], sem.at[len(copies)]))
    for copy in copies:
        copy.start()
    for copy in copies:
        copy.wait()


def pack(x, c, first, pieces, us):
    t, d = x.shape
    return pl.pallas_call(
        functools.partial(pack_kernel, first),
        out_shape=[jax.ShapeDtypeStruct((t, d // 2), jnp.bfloat16)] * pieces,
        in_specs=[pl.BlockSpec(memory_space=pl.ANY)] * 2,
        out_specs=[pl.BlockSpec(memory_space=pl.ANY)] * pieces,
        scratch_shapes=[pltpu.SemaphoreType.DMA((4 * pieces,))],
        compiler_params=params(),
        cost_estimate=cost(us),
        name="pack",
    )(x, c)


def weight_kernel(at, *refs):
    near, head, tail, grads, out = refs[:ROW], refs[ROW], refs[ROW + 1], refs[ROW + 2 : -1], refs[-1]
    t = near[0].shape[0]
    n, wide = out.shape[0] // 3, out.shape[1]
    left = jnp.concatenate([g[...] for g in grads], 1)

    def columns(first):
        parts = [near[0][:, at + first : at + first + wide], head[:, at + first : at + first + wide]]
        for i in range(1, ROW):
            parts.append(near[i][:, at + first : at + first + wide])
            parts.append(tail[(i - 1) * t : i * t, first : first + wide])
        return jnp.concatenate(parts)

    dot = functools.partial(jnp.dot, preferred_element_type=jnp.float32)
    out[: 2 * n] = dot(left[: 2 * n], columns(0)).astype(out.dtype)
    out[2 * n :] = dot(left[2 * n :], columns(wide)).astype(out.dtype)


def weight_terms(near, head, tail, grads, at, dtype, us):
    wide = near[0].shape[1] // 4
    return pl.pallas_call(
        functools.partial(weight_kernel, at * wide),
        out_shape=jax.ShapeDtypeStruct((grads[0].shape[0], wide), dtype),
        in_specs=[VMEM] * (2 * ROW + 2),
        out_specs=VMEM,
        compiler_params=params(),
        cost_estimate=cost(us),
        name="weight_terms",
    )(*near, head, tail, *grads)


def early_kernel(first, other, out):
    out[...] = (first[...] + other[...].astype(jnp.float32)).astype(out.dtype)


def early_sums(first, other):
    return pl.pallas_call(
        early_kernel,
        out_shape=jax.ShapeDtypeStruct(other.shape, jnp.bfloat16),
        in_specs=[VMEM] * 2,
        out_specs=VMEM,
        compiler_params=params(),
        cost_estimate=cost(0.5),
        name="early_sums",
    )(first, other)


def sum_kernel(first, second, second_other, gate, up, down):
    part = second.shape[0] // 3
    total = second[...] + second_other[...].astype(jnp.float32)
    for n, out in enumerate((gate, up, down)):
        out[:CUT] = first[n * CUT : (n + 1) * CUT]
        out[CUT:] = total[n * part : (n + 1) * part].astype(out.dtype)


def sums(first, second, second_other, s):
    return pl.pallas_call(
        sum_kernel,
        out_shape=[jax.ShapeDtypeStruct((s, first.shape[1]), jnp.bfloat16)] * 3,
        in_specs=[VMEM] * 3,
        out_specs=[VMEM] * 3,
        compiler_params=params(),
        cost_estimate=cost(1),
        name="sums",
    )(first, second, second_other)


def local(tokens, cotangent, gate_weight, up_weight, down_weight):
    w_gate, w_up, w_down = gate_weight.T, up_weight.T, down_weight
    s = w_gate.shape[0]
    t = tokens.shape[0]
    far_rows = along_blk(tokens, -1)
    in_hbm = [pltpu.with_memory_space_constraint(a, pltpu.HBM) for a in (tokens, cotangent)]
    near = [None, *pack(*in_hbm, 1, ROW - 1, 1)]
    late, near[1] = lax.optimization_barrier((cotangent, near[1]))
    far_cotan = along_blk(late, -1)
    near = [along_rep(near[i], 0, i) for i in range(1, ROW)]

    own = own_units(tokens, cotangent, w_gate, w_up, w_down, 20)
    own_x = row_term(*own, w_gate, w_up, 0, t, jnp.float32, 3)

    far_rows, own_x = lax.optimization_barrier((far_rows, own_x))
    gate, upval = gate_up(far_rows, w_gate, w_up, 2)
    first, second, both = far_units(far_cotan, w_down, gate, upval, *own, 1.5)
    far_x = row_term(first, second, w_gate, w_up, t, t, jnp.bfloat16, 1)
    near, far_x = lax.optimization_barrier((near, far_x))
    half = near[0].shape[1] // 2
    late, far_cotan = lax.optimization_barrier((cotangent, far_cotan))
    far_other = along_blk(jnp.concatenate([a[:, :half] for a in near]), -1)
    far_x = along_blk(far_x, 1)
    both = along_rep(both, 0, 3)
    first = [first, along_rep(first, 0, 1)]
    first += [along_rep(first[1], 0, 1), both[: 3 * CUT]]
    second = [second, along_rep(second, 0, 1), along_rep(both[3 * CUT :], 0, 3), both[3 * CUT :]]
    far_mine = along_blk(jnp.concatenate([a[:, half:] for a in near]), -1)
    far = pack(far_rows, far_cotan, 0, 1, 0.5)[0]
    near = [pack(tokens, late, 0, 1, 0.5)[0], *near]

    other = [along_rep(weight_terms(near, far, far_other, g, 0, jnp.bfloat16, 1), 1, 0) for g in (first, second)]
    mine = [weight_terms(near, far, far_mine, g, 2, jnp.float32, 1) for g in (first, second)]
    gate_grad, up_grad, down_grad = sums(early_sums(mine[0], other[0]), mine[1], other[1], s)
    input_grad = (own_x + far_x.astype(jnp.float32)).astype(jnp.bfloat16)
    return input_grad, gate_grad.T, up_grad.T, down_grad


def solution(mesh):
    in_specs = (
        P(("blk", "rep"), None),
        P(("blk", "rep"), None),
        P(None, "blk"),
        P(None, "blk"),
        P("blk", None),
    )
    out_specs = (P(("blk", "rep"), None), P("rep", "blk"), P("rep", "blk"), P("blk", "rep"))
    return jax.shard_map(local, mesh=mesh, in_specs=in_specs, out_specs=out_specs, check_vma=False)
```
